512 devices in a mesh: row: 32 (over y, z_lo), width: 16 (over x, z_hi, core).
Axes of the slice: x: 4, y: 4, z: 16 (z_hi: 2, z_lo: 8; z = z_hi * 8 + z_lo), core: 2. Of those that a mesh axis runs over, the one named last changes fastest.
Arguments:
- store: bfloat16 [16384, 65536], P('row', 'width')
- queries: bfloat16 [32, 96, 65536], P('row', None, 'width')
- owner: int32 [4], replicated, may hold values from 0 to 31
Outputs:
- scores: float32 [4, 96, 16384], P(None, 'width', 'row')
The draws below stay inside these ranges and needn't reach their ends.
Inputs may be any that keep to these rules, and one draw needn't show every extreme that they name: `owner`: index of a block of queries.
All inputs are finite; a program needn't handle non-finite values.
Results may differ from the reference program's by a relative error of at most 0.0003.
Values may be sent and summed in bfloat16 or wider, within the bound.
No kernel may reach another device: no remote copies, remote signals or barrier semaphores. Data moves between devices by JAX's collectives and lax.ppermute only.
A program may use at most 64 MiB of HBM per device.

```python
import math
import jax
import jax.numpy as jnp
from jax import lax

WIDTH = 65536
QB = 96
NBLK = 4
ROWS_DEV = 512
N_ROW = 32


def scaled_field(key, shape, top):
    base_key, row_key, col_key = jax.random.split(key, 3)
    base = jax.random.normal(base_key, shape, jnp.float32)
    row_shape = shape[:-1] + (1,)
    rows = jnp.exp(jax.random.uniform(row_key, row_shape, jnp.float32, 0.0, jnp.log(top)))
    cols = jnp.exp(jax.random.uniform(col_key, shape[-1:], jnp.float32, 0.0, jnp.log(top)))
    return base * rows * cols / top


def draw_store(key, part):
    key = jax.random.fold_in(key, 11)
    top = 10.0
    return scaled_field(key, (ROWS_DEV * N_ROW, WIDTH), top).astype(jnp.bfloat16)


def draw_queries(key, part):
    key = jax.random.fold_in(key, 23)
    top = 10.0
    return scaled_field(key, (N_ROW, QB, WIDTH), top).astype(jnp.bfloat16)


def plant(values, own_key, low, largest):
    spot = [jax.random.randint(jax.random.fold_in(own_key, axis), (), 0, length) for axis, length in enumerate(values.shape)]
    main_axis = values.shape.index(max(values.shape))
    neighbour = spot[:main_axis] + [(spot[main_axis] + 1) % values.shape[main_axis]] + spot[main_axis + 1:]
    return values.at[tuple(spot)].set(low).at[tuple(neighbour)].set(largest)


def setup_inputs(seed: int = 0) -> dict:
    splits = jax.random.split(jax.random.key(seed), 4)
    store = draw_store(jax.random.fold_in(splits[3], 71), 0)
    queries = draw_queries(jax.random.fold_in(splits[3], 71), 0)
    owner = plant(jax.random.randint(splits[2], (NBLK,), 0, N_ROW), jax.random.fold_in(splits[2], 1), 0, N_ROW - 1).astype(jnp.int32)
    return {"store": store, "queries": queries, "owner": owner}


def row_squares(block):
    return lax.optimization_barrier(jnp.sum(jnp.square(block.astype(jnp.float32)), axis=1))

def reference(store, queries, owner):
    shards = store.reshape(N_ROW, ROWS_DEV, WIDTH)
    store_sq = lax.map(row_squares, shards).reshape(ROWS_DEV * N_ROW)
    store_scale = lax.rsqrt(store_sq + 1e-06)
    results = []
    for index in range(NBLK):
        chosen = lax.dynamic_index_in_dim(queries, owner[index].astype(jnp.int32), 0, keepdims=False)
        inner = jnp.dot(chosen, store.T, preferred_element_type=jnp.float32)
        query_sq = row_squares(chosen)
        results.append(inner * lax.rsqrt(query_sq + 1e-06)[:, None] * store_scale[None, :] * math.sqrt(WIDTH))
    return jnp.stack(results)
```

```python
import math

import jax
import jax.numpy as jnp
from jax import lax
from jax.sharding import PartitionSpec as P

WIDTH = 65536
NY, NZ, NQ = 4, 8, 4
NX, NH, NC = 4, 2, 2
GROUPS_Y = [[y * NZ + z for y in range(NY)] for z in range(NZ)]
GROUPS_Q = [[y * NZ + h * NQ + k for k in range(NQ)] for y in range(NY) for h in range(2)]
GROUPS_XC = [[(x * NH + h) * NC + c for x in range(NX) for c in range(NC)] for h in range(NH)]
UP = [(y * NZ + z, (y + 1) % NY * NZ + z) for y in range(NY) for z in range(NZ)]
DOWN = [(b, a) for a, b in UP]
CROSS = [(r, r ^ NQ) for r in range(NY * NZ)]
SWAP_H = [(w, w ^ NC) for w in range(NX * NH * NC)]


def exchange(value, axis, groups):
    return lax.all_to_all(value, axis, 0, 0, axis_index_groups=groups)


def pick(parts, index):
    index = index.reshape((-1,) + (1,) * (parts.ndim - 2))
    out = parts[0]
    for k in range(1, parts.shape[0]):
        out = jnp.where(index == k, parts[k], out)
    return out


def spread(parts, owner, z):
    slots = owner.shape[0]
    _, rows, cols = parts.shape
    mine = pick(parts[:, None], owner // NZ)
    mine = mine.reshape(slots, NQ, rows // NQ, cols).transpose(1, 0, 2, 3)
    piece = pick(exchange(mine, "row", GROUPS_Q), owner % NQ)
    other = lax.ppermute(piece, "row", CROSS)
    here = (owner // NQ % 2 == z // NQ)[:, None, None]
    piece = jnp.where(here, piece, other)
    return exchange(jnp.broadcast_to(piece[None], (NQ,) + piece.shape), "row", GROUPS_Q)


def gather_y(mine):
    below = lax.ppermute(mine, "row", UP)
    above = lax.ppermute(mine, "row", DOWN)
    half = mine.shape[0] // 2
    far = jnp.concatenate(
        [lax.ppermute(below[:half], "row", UP), lax.ppermute(above[half:], "row", DOWN)]
    )
    return mine, below, above, far


def squares(block):
    return jnp.sum(jnp.square(block.astype(jnp.float32)), axis=-1)


def per_device(store, queries, owner):
    slots = owner.shape[0]
    rows, cols = queries.shape[1:]
    share = rows // (NX * NH * NC)
    y = lax.axis_index("row") // NZ
    z = lax.axis_index("row") % NZ
    quarter = cols // NY
    parts = queries[0].reshape(rows, NY, quarter).transpose(1, 0, 2)
    parts = exchange(parts, "row", GROUPS_Y)
    store_sq = squares(store)
    quarters = gather_y(spread(parts, owner, z))
    inner, query_sq = 0.0, 0.0
    for step, chosen in zip((0, -1, 1, 2), quarters):
        chosen = chosen.reshape(slots * rows, quarter)
        start = (y + step) % NY * quarter
        columns = lax.dynamic_slice_in_dim(store, start, quarter, 1)
        inner += lax.dot_general(
            chosen, columns, (((1,), (1,)), ((), ())), preferred_element_type=jnp.float32
        )
        query_sq += squares(chosen)
    def by_target(value):
        value = value.reshape(NX, slots, NH, NC, share, -1).transpose(0, 3, 2, 1, 4, 5)
        return value.reshape(NX * NC, NH, slots * share, -1)

    lanes = 128
    extra = jnp.zeros((slots * share, lanes), jnp.float32)
    extra = extra.at[:8, :64].set(store_sq.reshape(8, 64))
    extra = jnp.broadcast_to(extra, (NX * NC, NH, slots * share, lanes))
    extra = jnp.where(jnp.arange(lanes) == 64, by_target(query_sq), extra)
    total = jnp.concatenate([by_target(inner), extra], axis=3)
    total = jnp.sum(exchange(total, "width", GROUPS_XC), axis=0)
    h = lax.axis_index("width") // NC % NH
    keep = jnp.where(h == 0, total[0], total[1])
    give = jnp.where(h == 0, total[1], total[0])
    total = keep + lax.ppermute(give, "width", SWAP_H)
    depth = store.shape[0]
    store_sq = total[:8, depth : depth + 64].reshape(1, depth)
    query_sq = total[:, depth + 64 : depth + 65]
    scores = total[:, :depth] * lax.rsqrt(query_sq + 1e-06) * lax.rsqrt(store_sq + 1e-06)
    return (scores * math.sqrt(WIDTH)).reshape(slots, share, depth)


def solution(mesh):
    in_specs = (P("row", "width"), P("row", None, "width"), P())
    out_specs = P(None, "width", "row")
    return jax.shard_map(
        per_device, mesh=mesh, in_specs=in_specs, out_specs=out_specs, check_vma=False
    )
```

```python
import math

import jax
import jax.numpy as jnp
from jax import lax
from jax.experimental import pallas as pl
from jax.experimental.pallas import tpu as pltpu
from jax.sharding import PartitionSpec as P

WIDTH = 65536
NY, NZ, NQ = 4, 8, 4
NX, NH, NC = 4, 2, 2
NW = NX * NH * NC
EXTRA = 8
QUADS = [[y * NZ + h * NQ + k for k in range(NQ)] for y in range(NY) for h in range(2)]
SQUARES = [[y * NZ + h * NQ + k for y in range(NY) for k in range(NQ)] for h in range(2)]
PLANES = [
    [(y * NZ + z) * NW + (x * NH + h) * NC + c for y in range(NY) for x in range(NX)]
    for z in range(NZ) for h in range(NH) for c in range(NC)
]
CROSS = [(r, r ^ NQ) for r in range(NY * NZ)]
SWAP_C = [(w, w ^ 1) for w in range(NW)]
SWAP_H = [(w, w ^ NC) for w in range(NW)]


def turn(step):
    return [(y * NZ + z, (y + step) % NY * NZ + z) for y in range(NY) for z in range(NZ)]


def cut_kernel(block, out):
    width = out.shape[2]
    for part in range(out.shape[0]):
        out[part] = block[:, part * width : (part + 1) * width]


def cut_columns(block, parts):
    rows, cols = block.shape
    vmem = pl.BlockSpec(memory_space=pltpu.VMEM)
    return pl.pallas_call(
        cut_kernel,
        in_specs=[vmem],
        out_specs=vmem,
        out_shape=jax.ShapeDtypeStruct((parts, rows, cols // parts), block.dtype),
    )(block)


def products_kernel(y, chosen, store_sq, *refs):
    stores, (first, second), (blocks, done) = refs[:NY], refs[NY : NY + 2], refs[NY + 2 :]
    copies = [
        pltpu.make_async_copy(stores[step], blocks.at[step], done.at[step]) for step in range(NY)
    ]
    for copy in copies:
        copy.start()
    parts, rows, width = chosen.shape
    depth = store_sq.shape[1]
    few = second.shape[3]
    query_sq = jnp.zeros((EXTRA, rows), jnp.float32)
    ones = jnp.ones((EXTRA, width), jnp.bfloat16)
    for k in range(parts):
        square = jnp.square(chosen[k].astype(jnp.float32))
        high = square.astype(jnp.bfloat16)
        low = (square - high.astype(jnp.float32)).astype(jnp.bfloat16)
        for part in (high, low):
            query_sq += lax.dot_general(
                ones, part, (((1,), (1,)), ((), ())), preferred_element_type=jnp.float32
            )
    place = lax.broadcasted_iota(jnp.int32, (EXTRA, depth), 0)
    for step in range(NY):
        copies[step].wait()
        inner = 0.0
        for k in range(parts):
            inner += lax.dot_general(
                chosen[k], blocks[step, :, k * width : (k + 1) * width],
                (((1,), (1,)), ((), ())), preferred_element_type=jnp.float32,
            )
        target = lax.rem(y[0] + (NY - step), NY)
        for group, out in ((0, first), (1, second)):
            for side in range(NC):
                for x in range(NX):
                    at = ((group * NC + side) * NX + x) * few
                    out[side, pl.ds(target, 1), x, :few] = inner[None, at : at + few]
        for side in range(NC):
            for x in range(NX):
                extra = jnp.zeros((EXTRA, depth), jnp.float32)
                if step == 0:
                    extra = jnp.where(place == 0, store_sq[...], extra)
                for group in range(NH):
                    at = ((group * NC + side) * NX + x) * few
                    line = jnp.concatenate(
                        [query_sq[:, at : at + few], jnp.zeros((EXTRA, depth - few), jnp.float32)], axis=1
                    )
                    extra = jnp.where(place == group + 1, line, extra)
                first[side, pl.ds(target, 1), x, few:] = extra[None]


def products(y, chosen, store_sq, stores):
    parts, m, k = chosen.shape
    n = stores[0].shape[0]
    few = m // (NH * NC * NX)
    vmem = pl.BlockSpec(memory_space=pltpu.VMEM)
    return pl.pallas_call(
        products_kernel,
        in_specs=[pl.BlockSpec(memory_space=pltpu.SMEM), vmem, vmem]
        + [pl.BlockSpec(memory_space=pl.ANY)] * NY,
        out_specs=[vmem, vmem],
        out_shape=[
            jax.ShapeDtypeStruct((NC, NY, NX, few + EXTRA, n), jnp.float32),
            jax.ShapeDtypeStruct((NC, NY, NX, few, n), jnp.float32),
        ],
        scratch_shapes=[
            pltpu.VMEM((NY, n, parts * k), stores[0].dtype),
            pltpu.SemaphoreType.DMA((NY,)),
        ],
        compiler_params=pltpu.CompilerParams(vmem_limit_bytes=28 << 20),
        cost_estimate=pl.CostEstimate(
            flops=2 * NY * m * n * parts * k, bytes_accessed=NY * n * (parts * k * 2 + m * 4), transcendentals=0
        ),
    )(y.reshape(1), chosen, store_sq.reshape(1, n), *stores)


def squares(block):
    return jnp.sum(jnp.square(block.astype(jnp.float32)), axis=-1)


def per_device(store, queries, owner):
    slots = owner.shape[0]
    rows, cols = queries.shape[1:]
    depth = store.shape[0]
    share = rows // NW
    y = lax.axis_index("row") // NZ
    half = lax.axis_index("row") % NZ // NQ
    w = lax.axis_index("width")
    h, c = w // NC % NH, w % NC
    quarter = cols // NY
    parts = cut_columns(queries[0], NY * NQ)
    parts = lax.all_to_all(parts, "row", 0, 0, axis_index_groups=SQUARES)

    stores = []
    for step in range(NY):
        part = lax.dynamic_slice_in_dim(store, (y + step) % NY * quarter, quarter, 1)
        stores.append(lax.ppermute(part, "row", turn(step)) if step else part)

    row = jnp.arange(slots * rows)
    slot = row // share % slots
    x = row // (share * slots) % NX
    to_c = c ^ 1 ^ row // (share * slots * NX) % NC
    to_h = h ^ 1 ^ row // (share * slots * NX * NC)
    inside = ((x * NH + to_h) * NC + to_c) * share + row % share
    of_row = jnp.sum(jnp.where(slot[:, None] == jnp.arange(slots), owner, 0), axis=1)
    source = (of_row // NZ * NQ + of_row % NQ) * rows + inside
    one_hot = (source[:, None] == jnp.arange(NY * NQ * rows)).astype(parts.dtype)
    piece = jnp.dot(
        one_hot, parts.reshape(NY * NQ * rows, -1), preferred_element_type=jnp.float32
    ).astype(parts.dtype)
    other = lax.ppermute(piece, "row", CROSS)
    piece = jnp.where((of_row // NQ % 2 == half)[:, None], piece, other)
    chosen = lax.all_gather(piece, "row", axis_index_groups=QUADS)

    def summed(parts):
        give, keep = parts
        total = keep + lax.ppermute(give, "width", SWAP_C)
        total = total.reshape((NY * NX,) + total.shape[2:])
        total = lax.all_to_all(total, ("row", "width"), 0, 0, axis_index_groups=PLANES)
        return jnp.sum(total, axis=0)

    first, second = products(y, chosen, squares(store), stores)
    give, keep = summed(first), summed(second)
    few = slots * share
    got = lax.ppermute(give, "width", SWAP_H)
    total = keep + got[:few]
    store_sq = give[few] + got[few]
    query_sq = give[few + 2, :few] + got[few + 1, :few]
    scores = total * lax.rsqrt(query_sq + 1e-06)[:, None] * lax.rsqrt(store_sq + 1e-06)
    return (scores * math.sqrt(WIDTH)).reshape(slots, share, depth)


def solution(mesh):
    in_specs = (P("row", "width"), P("row", None, "width"), P())
    out_specs = P(None, "width", "row")
    return jax.shard_map(
        per_device, mesh=mesh, in_specs=in_specs, out_specs=out_specs, check_vma=False
    )
```

```python
import math

import jax
import jax.numpy as jnp
from jax import lax
from jax.experimental import pallas as pl
from jax.experimental.pallas import tpu as pltpu
from jax.sharding import PartitionSpec as P

WIDTH = 65536
NY, NZ, NQ = 4, 8, 4
NX, NH, NC = 4, 2, 2
NW = NX * NH * NC
LANES = 128
EXTRA = 8
QUADS = [[y * NZ + h * NQ + k for k in range(NQ)] for y in range(NY) for h in range(2)]
SQUARES = [[y * NZ + h * NQ + k for y in range(NY) for k in range(NQ)] for h in range(2)]
PLANES = [
    [(y * NZ + z) * NW + (x * NH + h) * NC + c for y in range(NY) for x in range(NX)]
    for z in range(NZ) for h in range(NH) for c in range(NC)
]
CROSS = [(r, r ^ NQ) for r in range(NY * NZ)]
SWAP_C = [(w, w ^ 1) for w in range(NW)]
SWAP_H = [(w, w ^ NC) for w in range(NW)]


def turn(step):
    return [(y * NZ + z, (y + step) % NY * NZ + z) for y in range(NY) for z in range(NZ)]


def cut_kernel(block, out):
    width = out.shape[2]
    for part in range(out.shape[0]):
        out[part] = block[:, part * width : (part + 1) * width]


def cut_columns(block, parts):
    rows, cols = block.shape
    vmem = pl.BlockSpec(memory_space=pltpu.VMEM)
    return pl.pallas_call(
        cut_kernel,
        in_specs=[vmem],
        out_specs=vmem,
        out_shape=jax.ShapeDtypeStruct((parts, rows, cols // parts), block.dtype),
    )(block)


def products_kernel(y, chosen, store_sq, *refs):
    stores, outs, (queries, blocks, done) = refs[:NY], refs[NY : NY + NH * NC], refs[NY + NH * NC :]
    copies = [pltpu.make_async_copy(chosen, queries, done.at[NY])] + [
        pltpu.make_async_copy(stores[step], blocks.at[step], done.at[step]) for step in range(NY)
    ]
    for copy in copies:
        copy.start()
    parts, rows, width = queries.shape
    few = rows // (NH * NC * NX)
    tiles = outs[-1].shape[2] // few
    copies[0].wait()
    query_sq = jnp.zeros((EXTRA, rows), jnp.float32)
    ones = jnp.ones((EXTRA, width), jnp.bfloat16)
    for k in range(parts):
        square = jnp.square(queries[k].astype(jnp.float32))
        high = square.astype(jnp.bfloat16)
        low = (square - high.astype(jnp.float32)).astype(jnp.bfloat16)
        for part in (high, low):
            query_sq += lax.dot_general(
                ones, part, (((1,), (1,)), ((), ())), preferred_element_type=jnp.float32
            )
    place = lax.broadcasted_iota(jnp.int32, (EXTRA, LANES), 0)
    for step in range(NY):
        copies[1 + step].wait()
        inner = 0.0
        for k in range(parts):
            inner += lax.dot_general(
                queries[k], blocks[step, :, k * width : (k + 1) * width],
                (((1,), (1,)), ((), ())), preferred_element_type=jnp.float32,
            )
        target = lax.rem(y[0] + (NY - step), NY)
        for side, out in enumerate(outs):
            for x in range(NX):
                at = (side * NX + x) * few
                for tile in range(tiles):
                    out[pl.ds(target, 1), x, tile * few : (tile + 1) * few] = inner[
                        None, at : at + few, tile * LANES : (tile + 1) * LANES
                    ]
        for side, out in enumerate(outs[:NC]):
            for x in range(NX):
                extra = store_sq[...] if step == 0 else jnp.zeros((EXTRA, LANES), jnp.float32)
                for group in range(NH):
                    at = ((group * NC + side) * NX + x) * few
                    line = jnp.concatenate(
                        [query_sq[:, at : at + few], jnp.zeros((EXTRA, LANES - few), jnp.float32)], axis=1
                    )
                    extra = jnp.where(place == tiles + group, line, extra)
                out[pl.ds(target, 1), x, tiles * few :] = extra[None]


def products(y, chosen, store_sq, stores):
    parts, m, k = chosen.shape
    n = stores[0].shape[0]
    few = m // (NH * NC * NX)
    height = n // LANES * few
    extra = jnp.pad(store_sq.reshape(n // LANES, LANES), ((0, EXTRA - n // LANES), (0, 0)))
    vmem, anywhere = pl.BlockSpec(memory_space=pltpu.VMEM), pl.BlockSpec(memory_space=pl.ANY)
    outs = pl.pallas_call(
        products_kernel,
        in_specs=[pl.BlockSpec(memory_space=pltpu.SMEM), anywhere, vmem] + [anywhere] * NY,
        out_specs=[vmem] * (NH * NC),
        out_shape=[
            jax.ShapeDtypeStruct((NY, NX, height + more, LANES), jnp.float32)
            for more in (EXTRA, 0) for _ in range(NC)
        ],
        scratch_shapes=[
            pltpu.VMEM((parts, m, k), chosen.dtype),
            pltpu.VMEM((NY, n, parts * k), stores[0].dtype),
            pltpu.SemaphoreType.DMA((NY + 1,)),
        ],
        compiler_params=pltpu.CompilerParams(vmem_limit_bytes=24 << 20),
        cost_estimate=pl.CostEstimate(
            flops=2 * NY * m * n * parts * k, bytes_accessed=NY * n * (parts * k * 2 + m * 4), transcendentals=0
        ),
    )(y.reshape(1), chosen, extra, *stores)
    return outs[:NC], outs[NC:]


def squares(block):
    return jnp.sum(jnp.square(block.astype(jnp.float32)), axis=-1)


def per_device(store, queries, owner):
    slots = owner.shape[0]
    rows, cols = queries.shape[1:]
    depth = store.shape[0]
    share = rows // NW
    y = lax.axis_index("row") // NZ
    half = lax.axis_index("row") % NZ // NQ
    w = lax.axis_index("width")
    h, c = w // NC % NH, w % NC
    quarter = cols // NY
    parts = cut_columns(queries[0], NY * NQ)
    parts = lax.all_to_all(parts, "row", 0, 0, axis_index_groups=SQUARES)

    stores = []
    for step in range(NY):
        part = lax.dynamic_slice_in_dim(store, (y + step) % NY * quarter, quarter, 1)
        stores.append(lax.ppermute(part, "row", turn(step)) if step else part)

    row = jnp.arange(slots * rows)
    slot = row % slots
    x = row // (share * slots) % NX
    to_c = c ^ 1 ^ row // (share * slots * NX) % NC
    to_h = h ^ 1 ^ row // (share * slots * NX * NC)
    inside = ((x * NH + to_h) * NC + to_c) * share + row // slots % share
    of_row = jnp.sum(jnp.where(slot[:, None] == jnp.arange(slots), owner, 0), axis=1)
    source = (of_row // NZ * NQ + of_row % NQ) * rows + inside
    one_hot = (source[:, None] == jnp.arange(NY * NQ * rows)).astype(parts.dtype)
    piece = jnp.dot(
        one_hot, parts.reshape(NY * NQ * rows, -1), preferred_element_type=jnp.float32
    ).astype(parts.dtype)
    other = lax.ppermute(piece, "row", CROSS)
    piece, store = lax.optimization_barrier((piece, store))
    store_sq = squares(store)
    piece = jnp.where((of_row // NQ % 2 == half)[:, None], piece, other)
    chosen = lax.all_gather(piece, "row", axis_index_groups=QUADS)

    def summed(parts):
        give, keep = parts
        total = keep + lax.ppermute(give, "width", SWAP_C)
        total = total.reshape((NY * NX,) + total.shape[2:])
        total = lax.all_to_all(total, ("row", "width"), 0, 0, axis_index_groups=PLANES)
        return jnp.sum(total, axis=0)

    first, second = products(y, chosen, store_sq, stores)
    give, keep = summed(first), summed(second)
    got = lax.ppermute(give, "width", SWAP_H)
    tiles, few = depth // LANES, slots * share
    height = tiles * few
    store_sq = (give + got)[height : height + tiles, None, None, :]
    query_sq = give[height + tiles + 1, :few] + got[height + tiles, :few]
    scores = (keep + got[:height]).reshape(tiles, share, slots, LANES)
    scores = scores * lax.rsqrt(query_sq + 1e-06).reshape(share, slots, 1)
    scores = scores * lax.rsqrt(store_sq + 1e-06) * math.sqrt(WIDTH)
    return scores.transpose(2, 1, 0, 3).reshape(slots, share, depth)


def solution(mesh):
    in_specs = (P("row", "width"), P("row", None, "width"), P())
    out_specs = P(None, "width", "row")
    return jax.shard_map(
        per_device, mesh=mesh, in_specs=in_specs, out_specs=out_specs, check_vma=False
    )
```

```python
import math

import jax
import jax.numpy as jnp
from jax import lax
from jax.experimental import pallas as pl
from jax.experimental.pallas import tpu as pltpu
from jax.sharding import PartitionSpec as P

WIDTH = 65536
NY, NZ, NQ = 4, 8, 4
NX, NH, NC = 4, 2, 2
NW = NX * NH * NC
LANES = 128
EXTRA = 8
QUADS = [[y * NZ + h * NQ + k for k in range(NQ)] for y in range(NY) for h in range(2)]
SQUARES = [[y * NZ + h * NQ + k for y in range(NY) for k in range(NQ)] for h in range(2)]
PLANES = [
    [(y * NZ + z) * NW + (x * NH + h) * NC + c for y in range(NY) for x in range(NX)]
    for z in range(NZ) for h in range(NH) for c in range(NC)
]
CROSS = [(r, r ^ NQ) for r in range(NY * NZ)]
SWAP_C = [(w, w ^ 1) for w in range(NW)]
SWAP_H = [(w, w ^ NC) for w in range(NW)]


def turn(step):
    return [(y * NZ + z, (y + step) % NY * NZ + z) for y in range(NY) for z in range(NZ)]


def cut_kernel(block, out, done):
    width = out.shape[2]
    copies = [
        pltpu.make_async_copy(block.at[:, pl.ds(part * width, width)], out.at[part], done.at[part])
        for part in range(out.shape[0])
    ]
    for copy in copies:
        copy.start()
    for copy in copies:
        copy.wait()


def cut_columns(block, parts):
    rows, cols = block.shape
    return pl.pallas_call(
        cut_kernel,
        in_specs=[pl.BlockSpec(memory_space=pl.ANY)],
        out_specs=pl.BlockSpec(memory_space=pltpu.VMEM),
        out_shape=jax.ShapeDtypeStruct((parts, rows, cols // parts), block.dtype),
        scratch_shapes=[pltpu.SemaphoreType.DMA((parts,))],
    )(block)


def products_kernel(y, chosen, store_sq, *refs):
    stores, outs, (queries, blocks, done) = refs[:NY], refs[NY : NY + NH * NC], refs[NY + NH * NC :]
    copies = [pltpu.make_async_copy(chosen, queries, done.at[NY])] + [
        pltpu.make_async_copy(stores[step], blocks.at[step], done.at[step]) for step in range(NY)
    ]
    for copy in copies:
        copy.start()
    parts, rows, width = queries.shape
    few = rows // (NH * NC * NX)
    tiles = outs[-1].shape[2] // few
    copies[0].wait()
    query_sq = jnp.zeros((EXTRA, rows), jnp.float32)
    ones = jnp.ones((EXTRA, width), jnp.bfloat16)
    for k in range(parts):
        square = jnp.square(queries[k].astype(jnp.float32))
        high = square.astype(jnp.bfloat16)
        low = (square - high.astype(jnp.float32)).astype(jnp.bfloat16)
        for part in (high, low):
            query_sq += lax.dot_general(
                ones, part, (((1,), (1,)), ((), ())), preferred_element_type=jnp.float32
            )
    place = lax.broadcasted_iota(jnp.int32, (EXTRA, LANES), 0)
    for step in range(NY):
        copies[1 + step].wait()
        inner = 0.0
        for k in range(parts):
            inner += lax.dot_general(
                queries[k], blocks[step, :, k * width : (k + 1) * width],
                (((1,), (1,)), ((), ())), preferred_element_type=jnp.float32,
            )
        target = lax.rem(y[0] + (NY - step), NY)
        for side, out in enumerate(outs):
            for x in range(NX):
                at = (side * NX + x) * few
                for tile in range(tiles):
                    out[pl.ds(target, 1), x, tile * few : (tile + 1) * few] = inner[
                        None, at : at + few, tile * LANES : (tile + 1) * LANES
                    ]
        for side, out in enumerate(outs[:NC]):
            for x in range(NX):
                extra = store_sq[...] if step == 0 else jnp.zeros((EXTRA, LANES), jnp.float32)
                for group in range(NH):
                    at = ((group * NC + side) * NX + x) * few
                    line = jnp.concatenate(
                        [query_sq[:, at : at + few], jnp.zeros((EXTRA, LANES - few), jnp.float32)], axis=1
                    )
                    extra = jnp.where(place == tiles + group, line, extra)
                out[pl.ds(target, 1), x, tiles * few :] = extra[None]


def products(y, chosen, store_sq, stores):
    parts, m, k = chosen.shape
    n = stores[0].shape[0]
    few = m // (NH * NC * NX)
    height = n // LANES * few
    extra = jnp.pad(store_sq.reshape(n // LANES, LANES), ((0, EXTRA - n // LANES), (0, 0)))
    vmem, anywhere = pl.BlockSpec(memory_space=pltpu.VMEM), pl.BlockSpec(memory_space=pl.ANY)
    outs = pl.pallas_call(
        products_kernel,
        in_specs=[pl.BlockSpec(memory_space=pltpu.SMEM), anywhere, vmem] + [anywhere] * NY,
        out_specs=[vmem] * (NH * NC),
        out_shape=[
            jax.ShapeDtypeStruct((NY, NX, height + more, LANES), jnp.float32)
            for more in (EXTRA, 0) for _ in range(NC)
        ],
        scratch_shapes=[
            pltpu.VMEM((parts, m, k), chosen.dtype),
            pltpu.VMEM((NY, n, parts * k), stores[0].dtype),
            pltpu.SemaphoreType.DMA((NY + 1,)),
        ],
        compiler_params=pltpu.CompilerParams(vmem_limit_bytes=24 << 20),
        cost_estimate=pl.CostEstimate(
            flops=2 * NY * m * n * parts * k, bytes_accessed=NY * n * (parts * k * 2 + m * 4), transcendentals=0
        ),
    )(y.reshape(1), chosen, extra, *stores)
    return outs[:NC], outs[NC:]


def squares(block):
    return jnp.sum(jnp.square(block.astype(jnp.float32)), axis=-1)


def per_device(store, queries, owner):
    slots = owner.shape[0]
    rows, cols = queries.shape[1:]
    depth = store.shape[0]
    share = rows // NW
    y = lax.axis_index("row") // NZ
    half = lax.axis_index("row") % NZ // NQ
    w = lax.axis_index("width")
    h, c = w // NC % NH, w % NC
    quarter = cols // NY
    parts = cut_columns(queries[0], NY * NQ)
    parts = lax.all_to_all(parts, "row", 0, 0, axis_index_groups=SQUARES)

    stores = []
    for step in range(NY):
        part = lax.dynamic_slice_in_dim(store, (y + step) % NY * quarter, quarter, 1)
        stores.append(lax.ppermute(part, "row", turn(step)) if step else part)

    row = jnp.arange(slots * rows)
    slot = row % slots
    x = row // (share * slots) % NX
    to_c = c ^ 1 ^ row // (share * slots * NX) % NC
    to_h = h ^ 1 ^ row // (share * slots * NX * NC)
    inside = ((x * NH + to_h) * NC + to_c) * share + row // slots % share
    of_row = jnp.sum(jnp.where(slot[:, None] == jnp.arange(slots), owner, 0), axis=1)
    source = (of_row // NZ * NQ + of_row % NQ) * rows + inside
    one_hot = (source[:, None] == jnp.arange(NY * NQ * rows)).astype(parts.dtype)
    piece = jnp.dot(
        one_hot, parts.reshape(NY * NQ * rows, -1), preferred_element_type=jnp.float32
    ).astype(parts.dtype)
    other = lax.ppermute(piece, "row", CROSS)
    piece, store = lax.optimization_barrier((piece, store))
    store_sq = squares(store)
    piece = jnp.where((of_row // NQ % 2 == half)[:, None], piece, other)
    chosen = lax.all_gather(piece, "row", axis_index_groups=QUADS)

    def summed(parts):
        give, keep = parts
        total = keep + lax.ppermute(give, "width", SWAP_C)
        total = total.reshape((NY * NX,) + total.shape[2:])
        total = lax.all_to_all(total, ("row", "width"), 0, 0, axis_index_groups=PLANES)
        return jnp.sum(total, axis=0)

    first, second = products(y, chosen, store_sq, stores)
    give, keep = summed(first), summed(second)
    got = lax.ppermute(give, "width", SWAP_H)
    tiles, few = depth // LANES, slots * share
    height = tiles * few
    store_sq = (give + got)[height : height + tiles, None, None, :]
    query_sq = give[height + tiles + 1, :few] + got[height + tiles, :few]
    scores = (keep + got[:height]).reshape(tiles, share, slots, LANES)
    scores = scores * lax.rsqrt(query_sq + 1e-06).reshape(share, slots, 1)
    scores = scores * lax.rsqrt(store_sq + 1e-06) * math.sqrt(WIDTH)
    return scores.transpose(2, 1, 0, 3).reshape(slots, share, depth)


def solution(mesh):
    in_specs = (P("row", "width"), P("row", None, "width"), P())
    out_specs = P(None, "width", "row")
    return jax.shard_map(
        per_device, mesh=mesh, in_specs=in_specs, out_specs=out_specs, check_vma=False
    )
```
